256 devices in a mesh: section: 2 (over y_hi), hid: 16 (over x, y_lo, core), wid: 8 (over z).
Axes of the slice: x: 4, y: 4 (y_hi: 2, y_lo: 2; y = y_hi * 2 + y_lo), z: 8, core: 2. Of those that a mesh axis runs over, the one named last changes fastest.
Arguments:
- w_first: bfloat16 [2, 5120, 20480], P('section', 'wid', 'hid'), may hold values from -0.078125 to 0.078125
- w_second: bfloat16 [2, 20480, 5120], P('section', 'hid', 'wid'), may hold values from -0.0390625 to 0.0390625
- saved_inputs: bfloat16 [2, 2, 256, 5120], P('section', None, None, 'wid'), may hold values from -0.75 to 0.75
- saved_hidden: bfloat16 [2, 2, 256, 20480], P('section', None, None, 'hid'), may hold values from -0.375 to 0.375
- cotangent: bfloat16 [2, 256, 5120], P(None, None, 'wid'), may hold values from -6 to 6
Outputs:
- grad_first: float32 [2, 5120, 20480], P('section', 'wid', 'hid')
- grad_second: float32 [2, 20480, 5120], P('section', 'hid', 'wid')
- input_grads: bfloat16 [2, 2, 256, 5120], P('section', None, 'hid', 'wid')
The draws below stay inside these ranges and needn't reach their ends.
All inputs are finite; a program needn't handle non-finite values.
Results may differ from the reference program's by a relative error of at most 0.0055.
Values may be sent and summed in bfloat16 or wider, within the bound.
A program may use at most 64 MiB of HBM per device.

```python
import jax
import jax.numpy as jnp

D = 5120
FF = 20480
ROWS = 256
MICRO = 2
SECTIONS = 2


def block_scale(key, extent, split, low, high):
    level = 1.0
    for dim, shards_of in split:
        steps = jax.random.uniform(jax.random.fold_in(jax.random.fold_in(key, 6), dim), (shards_of,), jnp.float32, low / len(split), high / len(split))
        level = level * jnp.repeat(jnp.exp(steps), extent[dim] // shards_of).reshape((-1,) + (1,) * (len(extent) - 1 - dim))
    return level


def bell_draw(own_key, shape, deviation, most, split=(), held_as=jnp.bfloat16):
    values = deviation * jax.random.normal(own_key, shape, jnp.float32)
    if split:
        values = values * block_scale(own_key, shape, split, -0.22, 0.18)
    return jnp.clip(values, -most, most).astype(held_as)


def setup_inputs(seed: int = 0) -> dict:
    seeds = jax.random.split(jax.random.key(seed), 6)
    w_first = bell_draw(seeds[0], (SECTIONS, D, FF), D ** -0.5, 0.078125, ((0, 2), (1, 8), (2, 16)))
    w_second = bell_draw(seeds[1], (SECTIONS, FF, D), FF ** -0.5, 0.0390625, ((0, 2), (1, 16), (2, 8)))
    saved_inputs = bell_draw(seeds[2], (SECTIONS, MICRO, ROWS, D), 0.125, 0.75, ((0, 2), (3, 8)))
    saved_hidden = bell_draw(seeds[3], (SECTIONS, MICRO, ROWS, FF), 0.0625, 0.375, ((0, 2), (3, 16)))
    cotangent = bell_draw(seeds[4], (MICRO, ROWS, D), 1.0, 6.0, ((2, 8),))
    return dict(w_first=w_first, w_second=w_second, saved_inputs=saved_inputs, saved_hidden=saved_hidden, cotangent=cotangent)


def layer_grads(inputs, pre_act, incoming, weight_first, weight_second):
    activated = jnp.maximum(pre_act, 0)
    summed = jnp.dot(incoming, weight_second.T, preferred_element_type=jnp.float32)
    hidden_grad = jnp.where(pre_act > 0, summed, jnp.float32(0.0)).astype(jnp.bfloat16)
    second = jnp.dot(activated.T, incoming, preferred_element_type=jnp.float32)
    first = jnp.dot(inputs.T, hidden_grad, preferred_element_type=jnp.float32)
    input_grad = jnp.dot(hidden_grad, weight_first.T, preferred_element_type=jnp.float32).astype(jnp.bfloat16)
    return first, second, input_grad


def reference(w_first, w_second, saved_inputs, saved_hidden, cotangent):
    first_sums = [jnp.zeros((D, FF), jnp.float32), jnp.zeros((D, FF), jnp.float32)]
    second_sums = [jnp.zeros((FF, D), jnp.float32), jnp.zeros((FF, D), jnp.float32)]
    results = [[None] * MICRO, [None] * MICRO]
    for micro_index in range(MICRO):
        incoming = cotangent[micro_index]
        for section_index in (1, 0):
            first, second, incoming = layer_grads(saved_inputs[section_index, micro_index], saved_hidden[section_index, micro_index], incoming, w_first[section_index], w_second[section_index])
            first_sums[section_index] = first_sums[section_index] + first
            second_sums[section_index] = second_sums[section_index] + second
            results[section_index][micro_index] = incoming
    grad_first = jnp.stack(first_sums)
    grad_second = jnp.stack(second_sums)
    input_grads = jnp.stack([jnp.stack(results[0]), jnp.stack(results[1])])
    return grad_first, grad_second, input_grads
```

```python
import functools

import jax
import jax.numpy as jnp
from jax import lax
from jax.experimental import pallas as pl
from jax.experimental.pallas import tpu as pltpu
from jax.sharding import PartitionSpec as P

MESH = pl.DeviceIdType.MESH
BF16 = jnp.bfloat16
F32 = jnp.float32

CHUNKS = 8
SPACING = 2
TILE = 16
SPLIT = 384


def nt_dot(a, b):
    return lax.dot_general(a, b, (((1,), (1,)), ((), ())), preferred_element_type=F32)


def tn_dot(a, b):
    return lax.dot_general(a, b, (((0,), (0,)), ((), ())), preferred_element_type=F32)


def relay_kernel(
    w_second_hbm, w_first_hbm, hidden_hbm, cotangent_hbm,
    incoming_out, hidden_grad_out, input_grad_out,
    w_second, w_first, pre, incoming, partial, step1_send, step1_land, step2_send, step2_land,
    gathered, share_send, share_own, share_land, rows_done,
    load_sem, store_sem, sum1_sem, sum2_sem, gather1_sem, gather2_sem, share_sem, relay_sem,
    sum1_sent, sum2_sent, gather1_sent, gather2_sent, share_sent, relay_sent,
):
    section = lax.axis_index("section")
    hid = lax.axis_index("hid")
    wid = lax.axis_index("wid")
    blocks = 4
    width = incoming.shape[-1]
    hid_count = 16
    wid_count = 8
    group = lax.div(hid, 4)
    member = lax.rem(hid, 4)

    def along(offset):
        return lax.rem(wid + (offset + wid_count), wid_count)

    def send(src, dst, sent, landed, target):
        pltpu.make_async_remote_copy(
            src_ref=src, dst_ref=dst, send_sem=sent, recv_sem=landed, device_id=target, device_id_type=MESH
        ).start()

    def wait_for(ref, sem):
        pltpu.make_async_copy(ref, ref, sem).wait()

    barrier = pltpu.get_barrier_semaphore()
    for offset in (1, -1, 2, -2):
        pl.semaphore_signal(barrier, inc=1, device_id=(section, hid, along(offset)), device_id_type=MESH)
    for offset in range(1, hid_count):
        pl.semaphore_signal(
            barrier, inc=1, device_id=(section, lax.rem(hid + offset, hid_count), wid), device_id_type=MESH
        )

    @pl.when(section == 0)
    def _():
        for other in range(hid_count):
            pl.semaphore_signal(barrier, inc=1, device_id=(1, other, wid), device_id_type=MESH)

    load_second = pltpu.make_async_copy(w_second_hbm, w_second, load_sem.at[0])
    load_first = pltpu.make_async_copy(w_first_hbm, w_first, load_sem.at[1])
    block = lax.rem(wid, blocks)
    half = lax.div(wid, blocks)
    load_pre = pltpu.make_async_copy(
        hidden_hbm.at[:, block, :, pl.ds(pl.multiple_of(half * width, 128), width)], pre, load_sem.at[2]
    )
    load_incoming = pltpu.make_async_copy(cotangent_hbm, incoming, load_sem.at[3])

    @pl.when(section == 1)
    def _():
        load_incoming.start()

    load_second.start()
    load_pre.start()
    load_first.start()

    @pl.when(section == 1)
    def _():
        load_incoming.wait()

    load_second.wait()
    load_pre.wait()
    load_first.wait()
    pl.semaphore_wait(barrier, 4 + hid_count - 1 + hid_count * section)

    def slot(c, piece):
        return lax.div(piece, blocks) * (CHUNKS * blocks) + c * blocks + lax.rem(piece, blocks)

    def phase_first_matmul(c):
        @pl.when(section == 0)
        def _():
            wait_for(incoming.at[c], relay_sem.at[c])

        rows = incoming[c].reshape(blocks * TILE, width)
        for h in range(2):
            product = nt_dot(rows, w_second[h * width : (h + 1) * width, :])
            for b in range(blocks):
                partial[c, h * blocks + b] = product[b * TILE : (b + 1) * TILE]
        for at, offset in enumerate((1, 3, -1, -3, 4)):
            step1_send[c, at] = partial[c, along(offset)].astype(BF16)
        sems = (sum1_sent.at[c], sum1_sem.at[c])
        send(
            step1_send.at[c, 4, :, pl.ds(0, SPLIT)], step1_land.at[c, 4, :, pl.ds(0, SPLIT)], *sems,
            (section, hid, along(2)),
        )
        send(
            step1_send.at[c, 4, :, pl.ds(SPLIT, width - SPLIT)], step1_land.at[c, 4, :, pl.ds(SPLIT, width - SPLIT)],
            *sems, (section, hid, along(-2)),
        )
        send(step1_send.at[c, pl.ds(0, 2)], step1_land.at[c, pl.ds(0, 2)], *sems, (section, hid, along(1)))
        send(step1_send.at[c, pl.ds(2, 2)], step1_land.at[c, pl.ds(2, 2)], *sems, (section, hid, along(-1)))

    def phase_collect(c):
        wait_for(step1_land.at[c], sum1_sem.at[c])
        up = partial[c, along(2)] + step1_land[c, 1].astype(F32)
        down = partial[c, along(-2)] + step1_land[c, 3].astype(F32)
        far = step1_land[c, 4].astype(F32)
        column = lax.broadcasted_iota(jnp.int32, far.shape, 1)
        zero = jnp.zeros_like(far)
        up = up + jnp.where(column < SPLIT, far, zero)
        down = down + jnp.where(column < SPLIT, zero, far)
        step2_send[c, 0] = up.astype(BF16)
        step2_send[c, 1] = down.astype(BF16)
        sems = (sum2_sent.at[c], sum2_sem.at[c])
        send(step2_send.at[c, 0], step2_land.at[c, 0], *sems, (section, hid, along(2)))
        send(step2_send.at[c, 1], step2_land.at[c, 1], *sems, (section, hid, along(-2)))

    def phase_finish_sum(c):
        own = partial[c, wid] + step1_land[c, 0].astype(F32) + step1_land[c, 2].astype(F32)
        wait_for(step2_land.at[c], sum2_sem.at[c])
        total = own + step2_land[c, 0].astype(F32) + step2_land[c, 1].astype(F32)
        mine = slot(c, wid)
        gathered[mine] = jnp.where(pre[c].astype(F32) > 0, total, jnp.zeros_like(total)).astype(BF16)
        for offset in (2, -2, 1, -1):
            send(
                gathered.at[mine], gathered.at[mine], gather1_sent.at[c], gather1_sem.at[c],
                (section, hid, along(offset)),
            )

    def phase_forward(c):
        wait_for(step1_land.at[c, pl.ds(0, 4)], gather1_sem.at[c])
        up = slot(c, along(2))
        down = slot(c, along(-2))
        sems = (gather2_sent.at[c], gather2_sem.at[c])
        send(
            gathered.at[up, :, pl.ds(0, SPLIT)], gathered.at[up, :, pl.ds(0, SPLIT)], *sems,
            (section, hid, along(-2)),
        )
        send(
            gathered.at[down, :, pl.ds(SPLIT, width - SPLIT)], gathered.at[down, :, pl.ds(SPLIT, width - SPLIT)], *sems,
            (section, hid, along(2)),
        )
        send(gathered.at[up], gathered.at[up], *sems, (section, hid, along(-1)))
        send(gathered.at[down], gathered.at[down], *sems, (section, hid, along(1)))

    def store_hidden_grad(c, h):
        at = pl.ds((h * CHUNKS + c) * blocks, blocks)
        return pltpu.make_async_copy(gathered.at[at], hidden_grad_out.at[at], store_sem.at[c, h])

    def phase_second_matmul(c):
        wait_for(step1_land.at[c, pl.ds(0, 3)], gather2_sem.at[c])
        product = None
        for h in range(2):
            grads = gathered[pl.ds((h * CHUNKS + c) * blocks, blocks)].reshape(blocks * TILE, width)
            term = nt_dot(grads, w_first[:, h * width : (h + 1) * width])
            product = term if product is None else product + term
        product = product.reshape(blocks, TILE, width)
        share_send[c] = product.astype(BF16)
        share_own[c] = product
        micro = lax.div(c, 4)
        owner_group = lax.rem(c, 4)
        for q in range(4):
            owner = owner_group * 4 + q

            @pl.when(owner != hid)
            def _():
                send(
                    share_send.at[c, q], share_land.at[micro, hid], share_sent.at[c], share_sem.at[micro],
                    (section, owner, wid),
                )

        for h in range(2):
            store_hidden_grad(c, h).start()

    def phase_finish_share(c):
        micro = lax.div(c, 4)

        @pl.when(lax.rem(c, 4) == group)
        def _():
            wait_for(share_land.at[micro, pl.ds(0, hid_count - 1)], share_sem.at[micro])

            def add(offset, total):
                return total + share_land[micro, lax.rem(hid + offset, hid_count)].astype(F32)

            total = lax.fori_loop(1, hid_count, add, share_own[c, member], unroll=True)
            rows_done[micro] = total.astype(BF16)

            @pl.when(section == 1)
            def _():
                for other in range(hid_count):
                    send(
                        rows_done.at[micro], incoming.at[c, member], relay_sent.at[micro], relay_sem.at[c],
                        (0, other, wid),
                    )

    phases = (
        phase_first_matmul, phase_collect, phase_finish_sum, phase_forward, phase_second_matmul, phase_finish_share,
    )

    def tick(t, carry):
        for index in reversed(range(len(phases))):
            c = t - SPACING * index

            @pl.when(jnp.logical_and(c >= 0, c < CHUNKS))
            def _():
                phases[index](c)

        return carry

    lax.fori_loop(0, CHUNKS + SPACING * (len(phases) - 1), tick, 0)

    store_rows = pltpu.make_async_copy(rows_done, input_grad_out, load_sem.at[0])
    store_rows.start()
    store_incoming = pltpu.make_async_copy(incoming, incoming_out, load_sem.at[1])
    store_incoming.start()

    def drain(c, carry):
        wait_for(step1_send.at[c], sum1_sent.at[c])
        wait_for(step2_send.at[c], sum2_sent.at[c])
        wait_for(step1_send.at[c, pl.ds(0, 4)], gather1_sent.at[c])
        wait_for(step1_send.at[c, pl.ds(0, 3)], gather2_sent.at[c])
        owner = lax.rem(c, 4) == group

        @pl.when(owner)
        def _():
            wait_for(share_send.at[c, pl.ds(0, 3)], share_sent.at[c])

            @pl.when(section == 1)
            def _():
                wait_for(share_land.at[0], relay_sent.at[lax.div(c, 4)])

        @pl.when(jnp.logical_not(owner))
        def _():
            wait_for(share_send.at[c], share_sent.at[c])

        for h in range(2):
            store_hidden_grad(c, h).wait()
        return carry

    lax.fori_loop(0, CHUNKS, drain, 0)
    store_rows.wait()
    store_incoming.wait()


def grads_kernel(inputs, grads, pre, incoming, rows, first, second, rows_out):
    width = inputs.shape[1]
    for h in range(2):
        first[:, h * incoming.shape[1] : (h + 1) * incoming.shape[1]] = tn_dot(inputs[...], grads[h])
    second[...] = tn_dot(jnp.maximum(pre[...], 0), incoming[...])
    rows_out[...] = rows[...]


def per_device(w_first, w_second, saved_inputs, saved_hidden, cotangent):
    w_first, w_second = w_first[0], w_second[0]
    width, units = w_first.shape
    micro_count, row_count = cotangent.shape[:2]
    rows = micro_count * row_count
    hidden = saved_hidden[0].reshape(rows, units)
    any_space = pl.BlockSpec(memory_space=pl.ANY)
    piece = (TILE, width)
    incoming, hidden_grad, input_grad = pl.pallas_call(
        relay_kernel,
        out_shape=(
            jax.ShapeDtypeStruct((CHUNKS, 4) + piece, BF16),
            jax.ShapeDtypeStruct((2 * CHUNKS * 4,) + piece, BF16),
            jax.ShapeDtypeStruct((2,) + piece, BF16),
        ),
        in_specs=[any_space] * 4,
        out_specs=(any_space,) * 3,
        scratch_shapes=[
            pltpu.VMEM((units, width), BF16),
            pltpu.VMEM((width, units), BF16),
            pltpu.VMEM((CHUNKS,) + piece, BF16),
            pltpu.VMEM((CHUNKS, 4) + piece, BF16),
            pltpu.VMEM((CHUNKS, 8) + piece, F32),
            pltpu.VMEM((CHUNKS, 5) + piece, BF16),
            pltpu.VMEM((CHUNKS, 5) + piece, BF16),
            pltpu.VMEM((CHUNKS, 2) + piece, BF16),
            pltpu.VMEM((CHUNKS, 2) + piece, BF16),
            pltpu.VMEM((2 * CHUNKS * 4,) + piece, BF16),
            pltpu.VMEM((CHUNKS, 4) + piece, BF16),
            pltpu.VMEM((CHUNKS, 4) + piece, F32),
            pltpu.VMEM((2, 16) + piece, BF16),
            pltpu.VMEM((2,) + piece, BF16),
            pltpu.SemaphoreType.DMA((4,)),
            pltpu.SemaphoreType.DMA((CHUNKS, 2)),
            pltpu.SemaphoreType.DMA((CHUNKS,)),
            pltpu.SemaphoreType.DMA((CHUNKS,)),
            pltpu.SemaphoreType.DMA((CHUNKS,)),
            pltpu.SemaphoreType.DMA((CHUNKS,)),
            pltpu.SemaphoreType.DMA((2,)),
            pltpu.SemaphoreType.DMA((CHUNKS,)),
            pltpu.SemaphoreType.DMA((CHUNKS,)),
            pltpu.SemaphoreType.DMA((CHUNKS,)),
            pltpu.SemaphoreType.DMA((CHUNKS,)),
            pltpu.SemaphoreType.DMA((CHUNKS,)),
            pltpu.SemaphoreType.DMA((CHUNKS,)),
            pltpu.SemaphoreType.DMA((2,)),
        ],
        compiler_params=pltpu.CompilerParams(
            collective_id=0, has_side_effects=True, vmem_limit_bytes=40 * 1024 * 1024
        ),
        name="relay",
    )(
        w_second,
        w_first,
        hidden.reshape(CHUNKS, 4, TILE, units),
        cotangent.reshape(CHUNKS, 4, TILE, width),
    )
    steps = 5
    first, second, input_grads = pl.pallas_call(
        grads_kernel,
        grid=(steps,),
        out_shape=(
            jax.ShapeDtypeStruct((width, units), F32),
            jax.ShapeDtypeStruct((units, width), F32),
            jax.ShapeDtypeStruct((2,) + piece, BF16),
        ),
        in_specs=[
            pl.BlockSpec((rows, width // steps), lambda i: (0, i)),
            pl.BlockSpec((2, rows, width), lambda i: (0, 0, 0)),
            pl.BlockSpec((rows, units // steps), lambda i: (0, i)),
            pl.BlockSpec((rows, width), lambda i: (0, 0)),
            pl.BlockSpec((2,) + piece, lambda i: (0, 0, 0)),
        ],
        out_specs=(
            pl.BlockSpec((width // steps, units), lambda i: (i, 0)),
            pl.BlockSpec((units // steps, width), lambda i: (i, 0)),
            pl.BlockSpec((2,) + piece, lambda i: (0, 0, 0)),
        ),
        compiler_params=pltpu.CompilerParams(vmem_limit_bytes=40 * 1024 * 1024),
        name="weight_grads",
    )(
        saved_inputs[0].reshape(rows, width),
        hidden_grad.reshape(2, rows, width),
        hidden,
        incoming.reshape(rows, width),
        input_grad,
    )
    return (first[None], second[None], input_grads[None])


def solution(mesh):
    placed = (
        P("section", "wid", "hid"),
        P("section", "hid", "wid"),
        P("section", None, None, "wid"),
        P("section", None, None, "hid"),
        P(None, None, "wid"),
    )
    return jax.shard_map(
        per_device,
        mesh=mesh,
        in_specs=placed,
        out_specs=(
            P("section", "wid", "hid"),
            P("section", "hid", "wid"),
            P("section", None, "hid", "wid"),
        ),
        check_vma=False,
    )
```

```python
import functools

import jax
import jax.numpy as jnp
from jax import lax
from jax.experimental import pallas as pl
from jax.experimental.pallas import tpu as pltpu
from jax.sharding import PartitionSpec as P

MESH = pl.DeviceIdType.MESH
BF16 = jnp.bfloat16
F32 = jnp.float32

CHUNKS = 8
CHUNK_TICKS = (3, 3)
PHASE_TICKS = (4, 4)
TILE = 16
SPLIT = 384


def dot(a, b):
    return jnp.dot(a, b, preferred_element_type=F32)


def transpose_into(dst, src, change=lambda x: x):
    count = src.shape[1] // 128

    def body(at, carry):
        part = pl.ds(pl.multiple_of(at * 128, 128), 128)
        dst[part, :] = change(src[:, part]).T
        return carry

    lax.fori_loop(0, count, body, 0)


def relay_kernel(
    w_second_hbm, w_first_hbm, hidden_hbm, cotangent_hbm, rows_hbm, inputs_hbm,
    incoming_out, hidden_grad_out, input_grad_out, activated_out, inputs_out,
    w_second_raw, w_first_raw, w_second, w_first, hidden_raw, inputs_raw, activated_t, inputs_t, pre, incoming, partial, step1_send, step1_land, step2_send, step2_land,
    gathered, share_send, share_own, share_land, rows_done,
    load_sem, store_sem, sum1_sem, sum2_sem, gather1_sem, gather2_sem, share_sem, relay_sem,
    sum1_sent, sum2_sent, gather1_sent, gather2_sent, share_sent, relay_sent,
):
    section = lax.axis_index("section")
    hid = lax.axis_index("hid")
    wid = lax.axis_index("wid")
    blocks = 4
    width = incoming.shape[-1]
    hid_count = 16
    wid_count = 8
    group = lax.div(hid, 4)
    member = lax.rem(hid, 4)

    def along(offset):
        return lax.rem(wid + (offset + wid_count), wid_count)

    def send(src, dst, sent, landed, target):
        pltpu.make_async_remote_copy(
            src_ref=src, dst_ref=dst, send_sem=sent, recv_sem=landed, device_id=target, device_id_type=MESH
        ).start()

    def wait_for(ref, sem):
        pltpu.make_async_copy(ref, ref, sem).wait()

    barrier = pltpu.get_barrier_semaphore()
    for offset in (1, -1, 2, -2):
        pl.semaphore_signal(barrier, inc=1, device_id=(section, hid, along(offset)), device_id_type=MESH)
    for offset in range(1, hid_count):
        pl.semaphore_signal(
            barrier, inc=1, device_id=(section, lax.rem(hid + offset, hid_count), wid), device_id_type=MESH
        )

    @pl.when(section == 0)
    def _():
        for other in range(hid_count):
            pl.semaphore_signal(barrier, inc=1, device_id=(1, other, wid), device_id_type=MESH)

    load_second = pltpu.make_async_copy(w_second_hbm, w_second_raw, load_sem.at[0])
    load_first = pltpu.make_async_copy(w_first_hbm, w_first_raw, load_sem.at[1])
    block = lax.rem(wid, blocks)
    half = lax.div(wid, blocks)
    load_pre = pltpu.make_async_copy(
        hidden_hbm.at[:, block, :, pl.ds(pl.multiple_of(half * width, 128), width)], pre, load_sem.at[2]
    )
    load_incoming = pltpu.make_async_copy(cotangent_hbm, incoming, load_sem.at[3])

    @pl.when(section == 1)
    def _():
        load_incoming.start()

    load_hidden = pltpu.make_async_copy(rows_hbm, hidden_raw, load_sem.at[4])
    load_inputs = pltpu.make_async_copy(inputs_hbm, inputs_raw, load_sem.at[5])
    store_activated = pltpu.make_async_copy(activated_t, activated_out, load_sem.at[4])
    store_inputs = pltpu.make_async_copy(inputs_t, inputs_out, load_sem.at[5])

    def transpose_rows():
        transpose_into(activated_t, hidden_raw, lambda x: jnp.maximum(x, 0))
        store_activated.start()
        transpose_into(inputs_t, inputs_raw)
        store_inputs.start()

    def first_matmul(c):
        rows = incoming[c].reshape(blocks * TILE, width)
        for h in range(2):
            product = dot(rows, w_second[:, h * width : (h + 1) * width])
            for b in range(blocks):
                partial[c, h * blocks + b] = product[b * TILE : (b + 1) * TILE]

    load_second.start()
    load_first.start()
    load_pre.start()
    load_hidden.start()
    load_inputs.start()
    load_second.wait()
    transpose_into(w_second, w_second_raw)

    @pl.when(section == 1)
    def _():
        load_incoming.wait()
        first_matmul(0)

    load_first.wait()
    transpose_into(w_first, w_first_raw)
    load_pre.wait()
    load_hidden.wait()
    load_inputs.wait()
    pl.semaphore_wait(barrier, 4 + hid_count - 1 + hid_count * section)

    @pl.when(section == 0)
    def _():
        transpose_rows()

    def slot(c, piece):
        return lax.div(piece, blocks) * (CHUNKS * blocks) + c * blocks + lax.rem(piece, blocks)

    def phase_first_matmul(c):
        @pl.when(section == 0)
        def _():
            wait_for(incoming.at[c], relay_sem.at[c])

        @pl.when(jnp.logical_or(section == 0, c > 0))
        def _():
            first_matmul(c)

        for at, offset in enumerate((1, 3, -1, -3, 4)):
            step1_send[c, at] = partial[c, along(offset)].astype(BF16)
        sems = (sum1_sent.at[c], sum1_sem.at[c])
        send(
            step1_send.at[c, 4, :, pl.ds(0, SPLIT)], step1_land.at[c, 4, :, pl.ds(0, SPLIT)], *sems,
            (section, hid, along(2)),
        )
        send(
            step1_send.at[c, 4, :, pl.ds(SPLIT, width - SPLIT)], step1_land.at[c, 4, :, pl.ds(SPLIT, width - SPLIT)],
            *sems, (section, hid, along(-2)),
        )
        send(step1_send.at[c, pl.ds(0, 2)], step1_land.at[c, pl.ds(0, 2)], *sems, (section, hid, along(1)))
        send(step1_send.at[c, pl.ds(2, 2)], step1_land.at[c, pl.ds(2, 2)], *sems, (section, hid, along(-1)))

    def phase_collect(c):
        wait_for(step1_land.at[c], sum1_sem.at[c])
        up = partial[c, along(2)] + step1_land[c, 1].astype(F32)
        down = partial[c, along(-2)] + step1_land[c, 3].astype(F32)
        far = step1_land[c, 4].astype(F32)
        column = lax.broadcasted_iota(jnp.int32, far.shape, 1)
        zero = jnp.zeros_like(far)
        up = up + jnp.where(column < SPLIT, far, zero)
        down = down + jnp.where(column < SPLIT, zero, far)
        step2_send[c, 0] = up.astype(BF16)
        step2_send[c, 1] = down.astype(BF16)
        sems = (sum2_sent.at[c], sum2_sem.at[c])
        send(step2_send.at[c, 0], step2_land.at[c, 0], *sems, (section, hid, along(2)))
        send(step2_send.at[c, 1], step2_land.at[c, 1], *sems, (section, hid, along(-2)))

    def phase_finish_sum(c):
        own = partial[c, wid] + step1_land[c, 0].astype(F32) + step1_land[c, 2].astype(F32)
        wait_for(step2_land.at[c], sum2_sem.at[c])
        total = own + step2_land[c, 0].astype(F32) + step2_land[c, 1].astype(F32)
        mine = slot(c, wid)
        gathered[mine] = jnp.where(pre[c].astype(F32) > 0, total, jnp.zeros_like(total)).astype(BF16)
        for offset in (2, -2, 1, -1):
            send(
                gathered.at[mine], gathered.at[mine], gather1_sent.at[c], gather1_sem.at[c],
                (section, hid, along(offset)),
            )

    def phase_forward(c):
        wait_for(step1_land.at[c, pl.ds(0, 4)], gather1_sem.at[c])
        up = slot(c, along(2))
        down = slot(c, along(-2))
        sems = (gather2_sent.at[c], gather2_sem.at[c])
        send(
            gathered.at[up, :, pl.ds(0, SPLIT)], gathered.at[up, :, pl.ds(0, SPLIT)], *sems,
            (section, hid, along(-2)),
        )
        send(
            gathered.at[down, :, pl.ds(SPLIT, width - SPLIT)], gathered.at[down, :, pl.ds(SPLIT, width - SPLIT)], *sems,
            (section, hid, along(2)),
        )
        send(gathered.at[up], gathered.at[up], *sems, (section, hid, along(-1)))
        send(gathered.at[down], gathered.at[down], *sems, (section, hid, along(1)))

    def store_hidden_grad(c, h):
        at = pl.ds((h * CHUNKS + c) * blocks, blocks)
        return pltpu.make_async_copy(gathered.at[at], hidden_grad_out.at[at], store_sem.at[c, h])

    def phase_second_matmul(c):
        wait_for(step1_land.at[c, pl.ds(0, 3)], gather2_sem.at[c])
        product = None
        for h in range(2):
            grads = gathered[pl.ds((h * CHUNKS + c) * blocks, blocks)].reshape(blocks * TILE, width)
            term = dot(grads, w_first[h * width : (h + 1) * width, :])
            product = term if product is None else product + term
        product = product.reshape(blocks, TILE, width)
        share_send[c] = product.astype(BF16)
        share_own[c] = product
        micro = lax.div(c, 4)
        owner_group = lax.rem(c, 4)
        for q in range(4):
            owner = owner_group * 4 + q

            @pl.when(owner != hid)
            def _():
                send(
                    share_send.at[c, q], share_land.at[micro, hid], share_sent.at[c], share_sem.at[micro],
                    (section, owner, wid),
                )

        for h in range(2):
            store_hidden_grad(c, h).start()

    def phase_finish_share(c):
        micro = lax.div(c, 4)

        @pl.when(lax.rem(c, 4) == group)
        def _():
            wait_for(share_land.at[micro, pl.ds(0, hid_count - 1)], share_sem.at[micro])

            def add(offset, total):
                return total + share_land[micro, lax.rem(hid + offset, hid_count)].astype(F32)

            total = lax.fori_loop(1, hid_count, add, share_own[c, member], unroll=True)
            rows_done[micro] = total.astype(BF16)

            @pl.when(section == 1)
            def _():
                for other in range(hid_count):
                    send(
                        rows_done.at[micro], incoming.at[c, member], relay_sent.at[micro], relay_sem.at[c],
                        (0, other, wid),
                    )

    phases = (
        phase_first_matmul, phase_collect, phase_finish_sum, phase_forward, phase_second_matmul, phase_finish_share,
    )

    chunk_ticks = jnp.where(section == 1, CHUNK_TICKS[1], CHUNK_TICKS[0])
    phase_ticks = jnp.where(section == 1, PHASE_TICKS[1], PHASE_TICKS[0])

    def tick(t, carry):
        for index in reversed(range(len(phases))):
            lag = t - phase_ticks * index
            c = lag // chunk_ticks

            @pl.when(jnp.logical_and(jnp.logical_and(c >= 0, c < CHUNKS), c * chunk_ticks == lag))
            def _():
                phases[index](c)

        return carry

    ticks = chunk_ticks * (CHUNKS - 1) + 1 + phase_ticks * (len(phases) - 1)
    lax.fori_loop(0, ticks, tick, 0)

    @pl.when(section == 1)
    def _():
        transpose_rows()

    store_rows = pltpu.make_async_copy(rows_done, input_grad_out, load_sem.at[0])
    store_rows.start()
    store_incoming = pltpu.make_async_copy(incoming, incoming_out, load_sem.at[1])
    store_incoming.start()

    def drain(c, carry):
        wait_for(step1_send.at[c], sum1_sent.at[c])
        wait_for(step2_send.at[c], sum2_sent.at[c])
        wait_for(step1_send.at[c, pl.ds(0, 4)], gather1_sent.at[c])
        wait_for(step1_send.at[c, pl.ds(0, 3)], gather2_sent.at[c])
        owner = lax.rem(c, 4) == group

        @pl.when(owner)
        def _():
            wait_for(share_send.at[c, pl.ds(0, 3)], share_sent.at[c])

            @pl.when(section == 1)
            def _():
                wait_for(share_land.at[0], relay_sent.at[lax.div(c, 4)])

        @pl.when(jnp.logical_not(owner))
        def _():
            wait_for(share_send.at[c], share_sent.at[c])

        for h in range(2):
            store_hidden_grad(c, h).wait()
        return carry

    lax.fori_loop(0, CHUNKS, drain, 0)
    store_rows.wait()
    store_incoming.wait()
    store_activated.wait()
    store_inputs.wait()


def grads_kernel(inputs, activated, incoming, grads, rows, first_out, second_out, rows_out, first, second, store_sem):
    width = incoming.shape[1]
    half = grads.shape[0] // 2
    part = 320
    stores = []

    def store(src, dst):
        stores.append(pltpu.make_async_copy(src, dst, store_sem.at[len(stores)]))
        stores[-1].start()

    for at in range(0, second.shape[0], part):
        at = pl.ds(at, part)
        second[at] = dot(activated[at], incoming[...])
        store(second.at[at], second_out.at[at])
    rows_out[...] = rows[...]
    for at in range(0, first.shape[0], part):
        at = pl.ds(at, part)
        for h in range(2):
            columns = pl.ds(h * width, width)
            first[at, columns] = dot(inputs[at], grads[h * half : (h + 1) * half])
            store(first.at[at, columns], first_out.at[at, columns])
    for copy in stores:
        copy.wait()


def per_device(w_first, w_second, saved_inputs, saved_hidden, cotangent):
    w_first, w_second = w_first[0], w_second[0]
    width, units = w_first.shape
    micro_count, row_count = cotangent.shape[:2]
    rows = micro_count * row_count
    hidden = saved_hidden[0].reshape(rows, units)
    any_space = pl.BlockSpec(memory_space=pl.ANY)
    piece = (TILE, width)
    inputs = saved_inputs[0].reshape(rows, width)
    incoming, hidden_grad, input_grad, activated_t, inputs_t = pl.pallas_call(
        relay_kernel,
        out_shape=(
            jax.ShapeDtypeStruct((CHUNKS, 4) + piece, BF16),
            jax.ShapeDtypeStruct((2 * CHUNKS * 4,) + piece, BF16),
            jax.ShapeDtypeStruct((2,) + piece, BF16),
            jax.ShapeDtypeStruct((units, rows), BF16),
            jax.ShapeDtypeStruct((width, rows), BF16),
        ),
        in_specs=[pl.BlockSpec(memory_space=pltpu.HBM)] * 6,
        out_specs=(any_space,) * 5,
        scratch_shapes=[
            pltpu.VMEM((units, width), BF16),
            pltpu.VMEM((width, units), BF16),
            pltpu.VMEM((width, units), BF16),
            pltpu.VMEM((units, width), BF16),
            pltpu.VMEM((rows, units), BF16),
            pltpu.VMEM((rows, width), BF16),
            pltpu.VMEM((units, rows), BF16),
            pltpu.VMEM((width, rows), BF16),
            pltpu.VMEM((CHUNKS,) + piece, BF16),
            pltpu.VMEM((CHUNKS, 4) + piece, BF16),
            pltpu.VMEM((CHUNKS, 8) + piece, F32),
            pltpu.VMEM((CHUNKS, 5) + piece, BF16),
            pltpu.VMEM((CHUNKS, 5) + piece, BF16),
            pltpu.VMEM((CHUNKS, 2) + piece, BF16),
            pltpu.VMEM((CHUNKS, 2) + piece, BF16),
            pltpu.VMEM((2 * CHUNKS * 4,) + piece, BF16),
            pltpu.VMEM((CHUNKS, 4) + piece, BF16),
            pltpu.VMEM((CHUNKS, 4) + piece, F32),
            pltpu.VMEM((2, 16) + piece, BF16),
            pltpu.VMEM((2,) + piece, BF16),
            pltpu.SemaphoreType.DMA((6,)),
            pltpu.SemaphoreType.DMA((CHUNKS, 2)),
            pltpu.SemaphoreType.DMA((CHUNKS,)),
            pltpu.SemaphoreType.DMA((CHUNKS,)),
            pltpu.SemaphoreType.DMA((CHUNKS,)),
            pltpu.SemaphoreType.DMA((CHUNKS,)),
            pltpu.SemaphoreType.DMA((2,)),
            pltpu.SemaphoreType.DMA((CHUNKS,)),
            pltpu.SemaphoreType.DMA((CHUNKS,)),
            pltpu.SemaphoreType.DMA((CHUNKS,)),
            pltpu.SemaphoreType.DMA((CHUNKS,)),
            pltpu.SemaphoreType.DMA((CHUNKS,)),
            pltpu.SemaphoreType.DMA((CHUNKS,)),
            pltpu.SemaphoreType.DMA((2,)),
        ],
        compiler_params=pltpu.CompilerParams(
            collective_id=0, has_side_effects=True, vmem_limit_bytes=32 * 1024 * 1024
        ),
        name="relay",
    )(
        *(
            pltpu.with_memory_space_constraint(array, pltpu.HBM)
            for array in (
                w_second,
                w_first,
                hidden.reshape(CHUNKS, 4, TILE, units),
                cotangent.reshape(CHUNKS, 4, TILE, width),
                hidden,
                inputs,
            )
        )
    )
    first, second, input_grads = pl.pallas_call(
        grads_kernel,
        out_shape=(
            jax.ShapeDtypeStruct((width, units), F32),
            jax.ShapeDtypeStruct((units, width), F32),
            jax.ShapeDtypeStruct((2,) + piece, BF16),
        ),
        in_specs=[pl.BlockSpec(memory_space=pltpu.VMEM)] * 5,
        out_specs=(any_space, any_space, pl.BlockSpec(memory_space=pltpu.VMEM)),
        scratch_shapes=[
            pltpu.VMEM((width, units), F32),
            pltpu.VMEM((units, width), F32),
            pltpu.SemaphoreType.DMA((8,)),
        ],
        compiler_params=pltpu.CompilerParams(vmem_limit_bytes=24 * 1024 * 1024),
        name="weight_grads",
    )(
        inputs_t,
        activated_t,
        incoming.reshape(rows, width),
        hidden_grad.reshape(2 * rows, width),
        input_grad,
    )
    return (first[None], second[None], input_grads[None])


def solution(mesh):
    placed = (
        P("section", "wid", "hid"),
        P("section", "hid", "wid"),
        P("section", None, None, "wid"),
        P("section", None, None, "hid"),
        P(None, None, "wid"),
    )
    return jax.shard_map(
        per_device,
        mesh=mesh,
        in_specs=placed,
        out_specs=(
            P("section", "wid", "hid"),
            P("section", "hid", "wid"),
            P("section", None, "hid", "wid"),
        ),
        check_vma=False,
    )
```

```python
import functools

import jax
import jax.numpy as jnp
from jax import lax
from jax.experimental import pallas as pl
from jax.experimental.pallas import tpu as pltpu
from jax.sharding import PartitionSpec as P

MESH = pl.DeviceIdType.MESH
BF16 = jnp.bfloat16
F32 = jnp.float32

CHUNKS = 8
ROUND = ((4, 5), (0, 0), (5, 6), (1, 1), (2, 2), (3, 3))
TILE = 16
SPLIT = 384


def dot(a, b):
    return jnp.dot(a, b, preferred_element_type=F32)


def transpose_into(dst, src, change=lambda x: x):
    count = src.shape[1] // 128

    def body(at, carry):
        part = pl.ds(pl.multiple_of(at * 128, 128), 128)
        dst[part, :] = change(src[:, part]).T
        return carry

    lax.fori_loop(0, count, body, 0)


def relay_kernel(
    w_second_hbm, w_first_hbm, hidden_hbm, cotangent_hbm, rows_hbm, inputs_hbm,
    incoming_out, hidden_grad_out, input_grad_out, activated_out, inputs_out,
    w_second_raw, w_first_raw, w_second, w_first, hidden_raw, inputs_raw, activated_t, inputs_t, pre, incoming, partial, step1_send, step1_land, step2_send, step2_land,
    gathered, share_send, share_own, share_land, rows_done,
    load_sem, store_sem, sum1_sem, sum2_sem, gather1_sem, gather2_sem, share_sem, relay_sem,
    sum1_sent, sum2_sent, gather1_sent, gather2_sent, share_sent, relay_sent,
):
    section = lax.axis_index("section")
    hid = lax.axis_index("hid")
    wid = lax.axis_index("wid")
    blocks = 4
    width = incoming.shape[-1]
    hid_count = 16
    wid_count = 8
    group = lax.div(hid, 4)
    member = lax.rem(hid, 4)

    def along(offset):
        return lax.rem(wid + (offset + wid_count), wid_count)

    def send(src, dst, sent, landed, target):
        pltpu.make_async_remote_copy(
            src_ref=src, dst_ref=dst, send_sem=sent, recv_sem=landed, device_id=target, device_id_type=MESH
        ).start()

    def wait_for(ref, sem):
        pltpu.make_async_copy(ref, ref, sem).wait()

    barrier = pltpu.get_barrier_semaphore()
    for offset in (1, -1, 2, -2):
        pl.semaphore_signal(barrier, inc=1, device_id=(section, hid, along(offset)), device_id_type=MESH)
    for offset in range(1, hid_count):
        pl.semaphore_signal(
            barrier, inc=1, device_id=(section, lax.rem(hid + offset, hid_count), wid), device_id_type=MESH
        )

    @pl.when(section == 0)
    def _():
        for other in range(hid_count):
            pl.semaphore_signal(barrier, inc=1, device_id=(1, other, wid), device_id_type=MESH)

    load_second = pltpu.make_async_copy(w_second_hbm, w_second_raw, load_sem.at[0])
    load_first = pltpu.make_async_copy(w_first_hbm, w_first_raw, load_sem.at[1])
    block = lax.rem(wid, blocks)
    half = lax.div(wid, blocks)
    load_pre = pltpu.make_async_copy(
        hidden_hbm.at[:, block, :, pl.ds(pl.multiple_of(half * width, 128), width)], pre, load_sem.at[2]
    )
    load_incoming = pltpu.make_async_copy(cotangent_hbm, incoming, load_sem.at[3])

    @pl.when(section == 1)
    def _():
        load_incoming.start()

    load_hidden = pltpu.make_async_copy(rows_hbm, hidden_raw, load_sem.at[4])
    load_inputs = pltpu.make_async_copy(inputs_hbm, inputs_raw, load_sem.at[5])
    store_activated = pltpu.make_async_copy(activated_t, activated_out, load_sem.at[4])
    store_inputs = pltpu.make_async_copy(inputs_t, inputs_out, load_sem.at[5])

    def transpose_rows():
        transpose_into(activated_t, hidden_raw, lambda x: jnp.maximum(x, 0))
        store_activated.start()
        transpose_into(inputs_t, inputs_raw)
        store_inputs.start()

    def first_matmul(c):
        rows = incoming[c].reshape(blocks * TILE, width)
        for h in range(2):
            product = dot(rows, w_second[:, h * width : (h + 1) * width])
            for b in range(blocks):
                partial[c, h * blocks + b] = product[b * TILE : (b + 1) * TILE]

    load_second.start()
    load_first.start()
    load_pre.start()
    load_hidden.start()
    load_inputs.start()
    load_second.wait()
    transpose_into(w_second, w_second_raw)

    @pl.when(section == 1)
    def _():
        load_incoming.wait()
        first_matmul(0)

    load_first.wait()
    transpose_into(w_first, w_first_raw)
    load_pre.wait()
    load_hidden.wait()
    load_inputs.wait()
    pl.semaphore_wait(barrier, 4 + hid_count - 1 + hid_count * section)

    @pl.when(section == 0)
    def _():
        transpose_rows()

    def slot(c, piece):
        return lax.div(piece, blocks) * (CHUNKS * blocks) + c * blocks + lax.rem(piece, blocks)

    def phase_first_matmul(c):
        @pl.when(section == 0)
        def _():
            wait_for(incoming.at[c], relay_sem.at[c])

        @pl.when(jnp.logical_or(section == 0, c > 0))
        def _():
            first_matmul(c)

        for at, offset in enumerate((1, 3, -1, -3, 4)):
            step1_send[c, at] = partial[c, along(offset)].astype(BF16)
        sems = (sum1_sent.at[c], sum1_sem.at[c])
        send(
            step1_send.at[c, 4, :, pl.ds(0, SPLIT)], step1_land.at[c, 4, :, pl.ds(0, SPLIT)], *sems,
            (section, hid, along(2)),
        )
        send(
            step1_send.at[c, 4, :, pl.ds(SPLIT, width - SPLIT)], step1_land.at[c, 4, :, pl.ds(SPLIT, width - SPLIT)],
            *sems, (section, hid, along(-2)),
        )
        send(step1_send.at[c, pl.ds(0, 2)], step1_land.at[c, pl.ds(0, 2)], *sems, (section, hid, along(1)))
        send(step1_send.at[c, pl.ds(2, 2)], step1_land.at[c, pl.ds(2, 2)], *sems, (section, hid, along(-1)))

    def phase_collect(c):
        wait_for(step1_land.at[c], sum1_sem.at[c])
        up = partial[c, along(2)] + step1_land[c, 1].astype(F32)
        down = partial[c, along(-2)] + step1_land[c, 3].astype(F32)
        far = step1_land[c, 4].astype(F32)
        column = lax.broadcasted_iota(jnp.int32, far.shape, 1)
        zero = jnp.zeros_like(far)
        up = up + jnp.where(column < SPLIT, far, zero)
        down = down + jnp.where(column < SPLIT, zero, far)
        step2_send[c, 0] = up.astype(BF16)
        step2_send[c, 1] = down.astype(BF16)
        sems = (sum2_sent.at[c], sum2_sem.at[c])
        send(step2_send.at[c, 0], step2_land.at[c, 0], *sems, (section, hid, along(2)))
        send(step2_send.at[c, 1], step2_land.at[c, 1], *sems, (section, hid, along(-2)))

    def phase_finish_sum(c):
        own = partial[c, wid] + step1_land[c, 0].astype(F32) + step1_land[c, 2].astype(F32)
        wait_for(step2_land.at[c], sum2_sem.at[c])
        total = own + step2_land[c, 0].astype(F32) + step2_land[c, 1].astype(F32)
        mine = slot(c, wid)
        gathered[mine] = jnp.where(pre[c].astype(F32) > 0, total, jnp.zeros_like(total)).astype(BF16)
        for offset in (2, -2, 1, -1):
            send(
                gathered.at[mine], gathered.at[mine], gather1_sent.at[c], gather1_sem.at[c],
                (section, hid, along(offset)),
            )

    def phase_forward(c):
        wait_for(step1_land.at[c, pl.ds(0, 4)], gather1_sem.at[c])
        up = slot(c, along(2))
        down = slot(c, along(-2))
        sems = (gather2_sent.at[c], gather2_sem.at[c])
        send(
            gathered.at[up, :, pl.ds(0, SPLIT)], gathered.at[up, :, pl.ds(0, SPLIT)], *sems,
            (section, hid, along(-2)),
        )
        send(
            gathered.at[down, :, pl.ds(SPLIT, width - SPLIT)], gathered.at[down, :, pl.ds(SPLIT, width - SPLIT)], *sems,
            (section, hid, along(2)),
        )
        send(gathered.at[up], gathered.at[up], *sems, (section, hid, along(-1)))
        send(gathered.at[down], gathered.at[down], *sems, (section, hid, along(1)))

    store_incoming = pltpu.make_async_copy(incoming, incoming_out, load_sem.at[1])

    def store_hidden_grad(c, h):
        at = pl.ds((h * CHUNKS + c) * blocks, blocks)
        return pltpu.make_async_copy(gathered.at[at], hidden_grad_out.at[at], store_sem.at[c, h])

    def phase_second_matmul(c):
        wait_for(step1_land.at[c, pl.ds(0, 3)], gather2_sem.at[c])
        product = None
        for h in range(2):
            grads = gathered[pl.ds((h * CHUNKS + c) * blocks, blocks)].reshape(blocks * TILE, width)
            term = dot(grads, w_first[h * width : (h + 1) * width, :])
            product = term if product is None else product + term
        product = product.reshape(blocks, TILE, width)
        share_send[c] = product.astype(BF16)
        share_own[c] = product
        micro = lax.div(c, 4)
        owner_group = lax.rem(c, 4)
        for q in range(4):
            owner = owner_group * 4 + q

            @pl.when(owner != hid)
            def _():
                send(
                    share_send.at[c, q], share_land.at[micro, hid], share_sent.at[c], share_sem.at[micro],
                    (section, owner, wid),
                )

        for h in range(2):
            store_hidden_grad(c, h).start()

        @pl.when(c == CHUNKS - 1)
        def _():
            store_incoming.start()

    def phase_finish_share(c):
        micro = lax.div(c, 4)

        @pl.when(lax.rem(c, 4) == group)
        def _():
            wait_for(share_land.at[micro, pl.ds(0, hid_count - 1)], share_sem.at[micro])

            def add(offset, total):
                return total + share_land[micro, lax.rem(hid + offset, hid_count)].astype(F32)

            total = lax.fori_loop(1, hid_count, add, share_own[c, member], unroll=True)
            rows_done[micro] = total.astype(BF16)

            @pl.when(section == 1)
            def _():
                for other in range(hid_count):
                    send(
                        rows_done.at[micro], incoming.at[c, member], relay_sent.at[micro], relay_sem.at[c],
                        (0, other, wid),
                    )

    phases = (
        phase_first_matmul, phase_collect, phase_finish_sum, phase_forward, phase_second_matmul, phase_finish_share,
    )

    def one_round(r, carry):
        for index, lag in ROUND:
            c = r - lag

            @pl.when(jnp.logical_and(c >= 0, c < CHUNKS))
            def _():
                phases[index](c)

        return carry

    lax.fori_loop(0, CHUNKS + max(lag for _, lag in ROUND), one_round, 0)

    @pl.when(section == 1)
    def _():
        transpose_rows()

    store_rows = pltpu.make_async_copy(rows_done, input_grad_out, load_sem.at[0])
    store_rows.start()

    def drain(c, carry):
        wait_for(step1_send.at[c], sum1_sent.at[c])
        wait_for(step2_send.at[c], sum2_sent.at[c])
        wait_for(step1_send.at[c, pl.ds(0, 4)], gather1_sent.at[c])
        wait_for(step1_send.at[c, pl.ds(0, 3)], gather2_sent.at[c])
        owner = lax.rem(c, 4) == group

        @pl.when(owner)
        def _():
            wait_for(share_send.at[c, pl.ds(0, 3)], share_sent.at[c])

            @pl.when(section == 1)
            def _():
                wait_for(share_land.at[0], relay_sent.at[lax.div(c, 4)])

        @pl.when(jnp.logical_not(owner))
        def _():
            wait_for(share_send.at[c], share_sent.at[c])

        for h in range(2):
            store_hidden_grad(c, h).wait()
        return carry

    lax.fori_loop(0, CHUNKS, drain, 0)
    store_rows.wait()
    store_incoming.wait()
    store_activated.wait()
    store_inputs.wait()


def grads_kernel(inputs, activated, incoming, grads, rows, first_out, second_out, rows_out, first, second, store_sem):
    width = incoming.shape[1]
    half = grads.shape[0] // 2
    part = 320
    stores = []

    def store(src, dst):
        stores.append(pltpu.make_async_copy(src, dst, store_sem.at[len(stores)]))
        stores[-1].start()

    for at in range(0, second.shape[0], part):
        at = pl.ds(at, part)
        second[at] = dot(activated[at], incoming[...])
        store(second.at[at], second_out.at[at])
    rows_out[...] = rows[...]
    for at in range(0, first.shape[0], part):
        at = pl.ds(at, part)
        for h in range(2):
            columns = pl.ds(h * width, width)
            first[at, columns] = dot(inputs[at], grads[h * half : (h + 1) * half])
            store(first.at[at, columns], first_out.at[at, columns])
    for copy in stores:
        copy.wait()


def per_device(w_first, w_second, saved_inputs, saved_hidden, cotangent):
    w_first, w_second = w_first[0], w_second[0]
    width, units = w_first.shape
    micro_count, row_count = cotangent.shape[:2]
    rows = micro_count * row_count
    hidden = saved_hidden[0].reshape(rows, units)
    any_space = pl.BlockSpec(memory_space=pl.ANY)
    piece = (TILE, width)
    inputs = saved_inputs[0].reshape(rows, width)
    incoming, hidden_grad, input_grad, activated_t, inputs_t = pl.pallas_call(
        relay_kernel,
        out_shape=(
            jax.ShapeDtypeStruct((CHUNKS, 4) + piece, BF16),
            jax.ShapeDtypeStruct((2 * CHUNKS * 4,) + piece, BF16),
            jax.ShapeDtypeStruct((2,) + piece, BF16),
            jax.ShapeDtypeStruct((units, rows), BF16),
            jax.ShapeDtypeStruct((width, rows), BF16),
        ),
        in_specs=[pl.BlockSpec(memory_space=pltpu.HBM)] * 6,
        out_specs=(any_space,) * 5,
        scratch_shapes=[
            pltpu.VMEM((units, width), BF16),
            pltpu.VMEM((width, units), BF16),
            pltpu.VMEM((width, units), BF16),
            pltpu.VMEM((units, width), BF16),
            pltpu.VMEM((rows, units), BF16),
            pltpu.VMEM((rows, width), BF16),
            pltpu.VMEM((units, rows), BF16),
            pltpu.VMEM((width, rows), BF16),
            pltpu.VMEM((CHUNKS,) + piece, BF16),
            pltpu.VMEM((CHUNKS, 4) + piece, BF16),
            pltpu.VMEM((CHUNKS, 8) + piece, F32),
            pltpu.VMEM((CHUNKS, 5) + piece, BF16),
            pltpu.VMEM((CHUNKS, 5) + piece, BF16),
            pltpu.VMEM((CHUNKS, 2) + piece, BF16),
            pltpu.VMEM((CHUNKS, 2) + piece, BF16),
            pltpu.VMEM((2 * CHUNKS * 4,) + piece, BF16),
            pltpu.VMEM((CHUNKS, 4) + piece, BF16),
            pltpu.VMEM((CHUNKS, 4) + piece, F32),
            pltpu.VMEM((2, 16) + piece, BF16),
            pltpu.VMEM((2,) + piece, BF16),
            pltpu.SemaphoreType.DMA((6,)),
            pltpu.SemaphoreType.DMA((CHUNKS, 2)),
            pltpu.SemaphoreType.DMA((CHUNKS,)),
            pltpu.SemaphoreType.DMA((CHUNKS,)),
            pltpu.SemaphoreType.DMA((CHUNKS,)),
            pltpu.SemaphoreType.DMA((CHUNKS,)),
            pltpu.SemaphoreType.DMA((2,)),
            pltpu.SemaphoreType.DMA((CHUNKS,)),
            pltpu.SemaphoreType.DMA((CHUNKS,)),
            pltpu.SemaphoreType.DMA((CHUNKS,)),
            pltpu.SemaphoreType.DMA((CHUNKS,)),
            pltpu.SemaphoreType.DMA((CHUNKS,)),
            pltpu.SemaphoreType.DMA((CHUNKS,)),
            pltpu.SemaphoreType.DMA((2,)),
        ],
        compiler_params=pltpu.CompilerParams(
            collective_id=0, has_side_effects=True, vmem_limit_bytes=32 * 1024 * 1024
        ),
        name="relay",
    )(
        *(
            pltpu.with_memory_space_constraint(array, pltpu.HBM)
            for array in (
                w_second,
                w_first,
                hidden.reshape(CHUNKS, 4, TILE, units),
                cotangent.reshape(CHUNKS, 4, TILE, width),
                hidden,
                inputs,
            )
        )
    )
    first, second, input_grads = pl.pallas_call(
        grads_kernel,
        out_shape=(
            jax.ShapeDtypeStruct((width, units), F32),
            jax.ShapeDtypeStruct((units, width), F32),
            jax.ShapeDtypeStruct((2,) + piece, BF16),
        ),
        in_specs=[pl.BlockSpec(memory_space=pltpu.VMEM)] * 5,
        out_specs=(any_space, any_space, pl.BlockSpec(memory_space=pltpu.VMEM)),
        scratch_shapes=[
            pltpu.VMEM((width, units), F32),
            pltpu.VMEM((units, width), F32),
            pltpu.SemaphoreType.DMA((8,)),
        ],
        compiler_params=pltpu.CompilerParams(vmem_limit_bytes=24 * 1024 * 1024),
        name="weight_grads",
    )(
        inputs_t,
        activated_t,
        incoming.reshape(rows, width),
        hidden_grad.reshape(2 * rows, width),
        input_grad,
    )
    return (first[None], second[None], input_grads[None])


def solution(mesh):
    placed = (
        P("section", "wid", "hid"),
        P("section", "hid", "wid"),
        P("section", None, None, "wid"),
        P("section", None, None, "hid"),
        P(None, None, "wid"),
    )
    return jax.shard_map(
        per_device,
        mesh=mesh,
        in_specs=placed,
        out_specs=(
            P("section", "wid", "hid"),
            P("section", "hid", "wid"),
            P("section", None, "hid", "wid"),
        ),
        check_vma=False,
    )
```

```python
import functools

import jax
import jax.numpy as jnp
from jax import lax
from jax.experimental import pallas as pl
from jax.experimental.pallas import tpu as pltpu
from jax.sharding import PartitionSpec as P

MESH = pl.DeviceIdType.MESH
BF16 = jnp.bfloat16
F32 = jnp.float32

CHUNKS = 8
ROUND = ((4, 5), (0, 0), (5, 6), (1, 1), (2, 2), (3, 3))
TILE = 16
SPLIT = 384


def dot(a, b):
    return jnp.dot(a, b, preferred_element_type=F32)


def transpose_into(dst, src, change=lambda x: x):
    count = src.shape[1] // 128

    def body(at, carry):
        part = pl.ds(pl.multiple_of(at * 128, 128), 128)
        dst[part, :] = change(src[:, part]).T
        return carry

    lax.fori_loop(0, count, body, 0)


def relay_kernel(
    w_second_hbm, w_first_hbm, hidden_hbm, cotangent_hbm, rows_hbm, inputs_hbm,
    incoming_out, hidden_grad_out, input_grad_out, activated_out, inputs_out,
    w_second_raw, w_first_raw, w_second, w_first, hidden_raw, inputs_raw, activated_t, inputs_t, pre, incoming, partial, step1_send, step1_land, step2_send, step2_land,
    gathered, share_send, share_own, share_land, rows_done,
    load_sem, store_sem, sum1_sem, sum2_sem, gather1_sem, gather2_sem, share_sem, relay_sem,
    sum1_sent, sum2_sent, gather1_sent, gather2_sent, share_sent, relay_sent,
):
    section = lax.axis_index("section")
    hid = lax.axis_index("hid")
    wid = lax.axis_index("wid")
    blocks = 4
    width = incoming.shape[-1]
    hid_count = 16
    wid_count = 8
    group = lax.div(hid, 4)
    member = lax.rem(hid, 4)

    def along(offset):
        return lax.rem(wid + (offset + wid_count), wid_count)

    def send(src, dst, sent, landed, target):
        pltpu.make_async_remote_copy(
            src_ref=src, dst_ref=dst, send_sem=sent, recv_sem=landed, device_id=target, device_id_type=MESH
        ).start()

    def wait_for(ref, sem):
        pltpu.make_async_copy(ref, ref, sem).wait()

    barrier = pltpu.get_barrier_semaphore()
    for offset in (1, -1, 2, -2):
        pl.semaphore_signal(barrier, inc=1, device_id=(section, hid, along(offset)), device_id_type=MESH)
    for offset in range(1, hid_count):
        pl.semaphore_signal(
            barrier, inc=1, device_id=(section, lax.rem(hid + offset, hid_count), wid), device_id_type=MESH
        )

    @pl.when(section == 0)
    def _():
        for other in range(hid_count):
            pl.semaphore_signal(barrier, inc=1, device_id=(1, other, wid), device_id_type=MESH)

    load_second = pltpu.make_async_copy(w_second_hbm, w_second_raw, load_sem.at[0])
    load_first = pltpu.make_async_copy(w_first_hbm, w_first_raw, load_sem.at[1])
    block = lax.rem(wid, blocks)
    half = lax.div(wid, blocks)
    load_pre = pltpu.make_async_copy(
        hidden_hbm.at[:, block, :, pl.ds(pl.multiple_of(half * width, 128), width)], pre, load_sem.at[2]
    )
    load_incoming = pltpu.make_async_copy(cotangent_hbm, incoming, load_sem.at[3])

    @pl.when(section == 1)
    def _():
        load_incoming.start()

    load_hidden = pltpu.make_async_copy(rows_hbm, hidden_raw, load_sem.at[4])
    load_inputs = pltpu.make_async_copy(inputs_hbm, inputs_raw, load_sem.at[5])
    store_activated = pltpu.make_async_copy(activated_t, activated_out, load_sem.at[4])
    store_inputs = pltpu.make_async_copy(inputs_t, inputs_out, load_sem.at[5])

    def transpose_rows():
        transpose_into(activated_t, hidden_raw, lambda x: jnp.maximum(x, 0))
        store_activated.start()
        transpose_into(inputs_t, inputs_raw)
        store_inputs.start()

    def first_matmul(c):
        rows = incoming[c].reshape(blocks * TILE, width)
        for h in range(2):
            product = dot(rows, w_second[:, h * width : (h + 1) * width])
            for b in range(blocks):
                partial[c, h * blocks + b] = product[b * TILE : (b + 1) * TILE]

    load_second.start()
    load_first.start()
    load_pre.start()
    load_hidden.start()
    load_inputs.start()
    load_second.wait()
    transpose_into(w_second, w_second_raw)

    @pl.when(section == 1)
    def _():
        load_incoming.wait()
        first_matmul(0)

    load_first.wait()
    transpose_into(w_first, w_first_raw)
    load_pre.wait()
    load_hidden.wait()
    load_inputs.wait()
    pl.semaphore_wait(barrier, 4 + hid_count - 1 + hid_count * section)

    @pl.when(section == 0)
    def _():
        transpose_rows()

    def slot(c, piece):
        return lax.div(piece, blocks) * (CHUNKS * blocks) + c * blocks + lax.rem(piece, blocks)

    def phase_first_matmul(c):
        @pl.when(section == 0)
        def _():
            wait_for(incoming.at[c], relay_sem.at[c])

        @pl.when(jnp.logical_or(section == 0, c > 0))
        def _():
            first_matmul(c)

        for at, offset in enumerate((1, 3, -1, -3, 4)):
            step1_send[c, at] = partial[c, along(offset)].astype(BF16)
        sems = (sum1_sent.at[c], sum1_sem.at[c])
        send(
            step1_send.at[c, 4, :, pl.ds(0, SPLIT)], step1_land.at[c, 4, :, pl.ds(0, SPLIT)], *sems,
            (section, hid, along(2)),
        )
        send(
            step1_send.at[c, 4, :, pl.ds(SPLIT, width - SPLIT)], step1_land.at[c, 4, :, pl.ds(SPLIT, width - SPLIT)],
            *sems, (section, hid, along(-2)),
        )
        send(step1_send.at[c, pl.ds(0, 2)], step1_land.at[c, pl.ds(0, 2)], *sems, (section, hid, along(1)))
        send(step1_send.at[c, pl.ds(2, 2)], step1_land.at[c, pl.ds(2, 2)], *sems, (section, hid, along(-1)))

    def phase_collect(c):
        wait_for(step1_land.at[c], sum1_sem.at[c])
        up = partial[c, along(2)] + step1_land[c, 1].astype(F32)
        down = partial[c, along(-2)] + step1_land[c, 3].astype(F32)
        far = step1_land[c, 4].astype(F32)
        column = lax.broadcasted_iota(jnp.int32, far.shape, 1)
        zero = jnp.zeros_like(far)
        up = up + jnp.where(column < SPLIT, far, zero)
        down = down + jnp.where(column < SPLIT, zero, far)
        step2_send[c, 0] = up.astype(BF16)
        step2_send[c, 1] = down.astype(BF16)
        sems = (sum2_sent.at[c], sum2_sem.at[c])
        send(step2_send.at[c, 0], step2_land.at[c, 0], *sems, (section, hid, along(2)))
        send(step2_send.at[c, 1], step2_land.at[c, 1], *sems, (section, hid, along(-2)))

    def phase_finish_sum(c):
        own = partial[c, wid] + step1_land[c, 0].astype(F32) + step1_land[c, 2].astype(F32)
        wait_for(step2_land.at[c], sum2_sem.at[c])
        total = own + step2_land[c, 0].astype(F32) + step2_land[c, 1].astype(F32)
        mine = slot(c, wid)
        gathered[mine] = jnp.where(pre[c].astype(F32) > 0, total, jnp.zeros_like(total)).astype(BF16)
        for offset in (2, -2, 1, -1):
            send(
                gathered.at[mine], gathered.at[mine], gather1_sent.at[c], gather1_sem.at[c],
                (section, hid, along(offset)),
            )

    def phase_forward(c):
        wait_for(step1_land.at[c, pl.ds(0, 4)], gather1_sem.at[c])
        up = slot(c, along(2))
        down = slot(c, along(-2))
        sems = (gather2_sent.at[c], gather2_sem.at[c])
        send(
            gathered.at[up, :, pl.ds(0, SPLIT)], gathered.at[up, :, pl.ds(0, SPLIT)], *sems,
            (section, hid, along(-2)),
        )
        send(
            gathered.at[down, :, pl.ds(SPLIT, width - SPLIT)], gathered.at[down, :, pl.ds(SPLIT, width - SPLIT)], *sems,
            (section, hid, along(2)),
        )
        send(gathered.at[up], gathered.at[up], *sems, (section, hid, along(-1)))
        send(gathered.at[down], gathered.at[down], *sems, (section, hid, along(1)))

    store_incoming = pltpu.make_async_copy(incoming, incoming_out, load_sem.at[1])

    def store_hidden_grad(c, h):
        at = pl.ds((h * CHUNKS + c) * blocks, blocks)
        return pltpu.make_async_copy(gathered.at[at], hidden_grad_out.at[at], store_sem.at[c, h])

    def drain(c, carry):
        wait_for(step1_send.at[c], sum1_sent.at[c])
        wait_for(step2_send.at[c], sum2_sent.at[c])
        wait_for(step1_send.at[c, pl.ds(0, 4)], gather1_sent.at[c])
        wait_for(step1_send.at[c, pl.ds(0, 3)], gather2_sent.at[c])
        owner = lax.rem(c, 4) == group

        @pl.when(owner)
        def _():
            wait_for(share_send.at[c, pl.ds(0, 3)], share_sent.at[c])

            @pl.when(section == 1)
            def _():
                wait_for(share_land.at[0], relay_sent.at[lax.div(c, 4)])

        @pl.when(jnp.logical_not(owner))
        def _():
            wait_for(share_send.at[c], share_sent.at[c])

        for h in range(2):
            store_hidden_grad(c, h).wait()
        return carry

    def phase_second_matmul(c):
        wait_for(step1_land.at[c, pl.ds(0, 3)], gather2_sem.at[c])
        product = None
        for h in range(2):
            grads = gathered[pl.ds((h * CHUNKS + c) * blocks, blocks)].reshape(blocks * TILE, width)
            term = dot(grads, w_first[h * width : (h + 1) * width, :])
            product = term if product is None else product + term
        product = product.reshape(blocks, TILE, width)
        share_send[c] = product.astype(BF16)
        share_own[c] = product
        micro = lax.div(c, 4)
        owner_group = lax.rem(c, 4)
        for q in range(4):
            owner = owner_group * 4 + q

            @pl.when(owner != hid)
            def _():
                send(
                    share_send.at[c, q], share_land.at[micro, hid], share_sent.at[c], share_sem.at[micro],
                    (section, owner, wid),
                )

        for h in range(2):
            store_hidden_grad(c, h).start()

        @pl.when(c == CHUNKS - 1)
        def _():
            store_incoming.start()
            lax.fori_loop(0, CHUNKS - 2, drain, 0)

    def phase_finish_share(c):
        micro = lax.div(c, 4)

        @pl.when(lax.rem(c, 4) == group)
        def _():
            wait_for(share_land.at[micro, pl.ds(0, hid_count - 1)], share_sem.at[micro])

            def add(offset, total):
                return total + share_land[micro, lax.rem(hid + offset, hid_count)].astype(F32)

            total = lax.fori_loop(1, hid_count, add, share_own[c, member], unroll=True)
            rows_done[micro] = total.astype(BF16)

            @pl.when(section == 1)
            def _():
                for other in range(hid_count):
                    send(
                        rows_done.at[micro], incoming.at[c, member], relay_sent.at[micro], relay_sem.at[c],
                        (0, other, wid),
                    )

    phases = (
        phase_first_matmul, phase_collect, phase_finish_sum, phase_forward, phase_second_matmul, phase_finish_share,
    )

    def one_round(r, carry):
        for index, lag in ROUND:
            c = r - lag

            @pl.when(jnp.logical_and(c >= 0, c < CHUNKS))
            def _():
                phases[index](c)

        return carry

    lax.fori_loop(0, CHUNKS + max(lag for _, lag in ROUND), one_round, 0)

    @pl.when(section == 1)
    def _():
        transpose_rows()

    store_rows = pltpu.make_async_copy(rows_done, input_grad_out, load_sem.at[0])
    store_rows.start()

    lax.fori_loop(CHUNKS - 2, CHUNKS, drain, 0)
    store_rows.wait()
    store_incoming.wait()
    store_activated.wait()
    store_inputs.wait()


def grads_kernel(inputs, activated, incoming, grads, rows, first_out, second_out, rows_out, first, second, store_sem):
    width = incoming.shape[1]
    half = grads.shape[0] // 2
    part = 320
    stores = []

    def store(src, dst):
        stores.append(pltpu.make_async_copy(src, dst, store_sem.at[len(stores)]))
        stores[-1].start()

    for at in range(0, second.shape[0], part):
        at = pl.ds(at, part)
        second[at] = dot(activated[at], incoming[...])
        store(second.at[at], second_out.at[at])
    rows_out[...] = rows[...]
    for at in range(0, first.shape[0], part):
        at = pl.ds(at, part)
        for h in range(2):
            columns = pl.ds(h * width, width)
            first[at, columns] = dot(inputs[at], grads[h * half : (h + 1) * half])
            store(first.at[at, columns], first_out.at[at, columns])
    for copy in stores:
        copy.wait()


def per_device(w_first, w_second, saved_inputs, saved_hidden, cotangent):
    w_first, w_second = w_first[0], w_second[0]
    width, units = w_first.shape
    micro_count, row_count = cotangent.shape[:2]
    rows = micro_count * row_count
    hidden = saved_hidden[0].reshape(rows, units)
    any_space = pl.BlockSpec(memory_space=pl.ANY)
    piece = (TILE, width)
    inputs = saved_inputs[0].reshape(rows, width)
    incoming, hidden_grad, input_grad, activated_t, inputs_t = pl.pallas_call(
        relay_kernel,
        out_shape=(
            jax.ShapeDtypeStruct((CHUNKS, 4) + piece, BF16),
            jax.ShapeDtypeStruct((2 * CHUNKS * 4,) + piece, BF16),
            jax.ShapeDtypeStruct((2,) + piece, BF16),
            jax.ShapeDtypeStruct((units, rows), BF16),
            jax.ShapeDtypeStruct((width, rows), BF16),
        ),
        in_specs=[pl.BlockSpec(memory_space=pltpu.HBM)] * 6,
        out_specs=(any_space,) * 5,
        scratch_shapes=[
            pltpu.VMEM((units, width), BF16),
            pltpu.VMEM((width, units), BF16),
            pltpu.VMEM((width, units), BF16),
            pltpu.VMEM((units, width), BF16),
            pltpu.VMEM((rows, units), BF16),
            pltpu.VMEM((rows, width), BF16),
            pltpu.VMEM((units, rows), BF16),
            pltpu.VMEM((width, rows), BF16),
            pltpu.VMEM((CHUNKS,) + piece, BF16),
            pltpu.VMEM((CHUNKS, 4) + piece, BF16),
            pltpu.VMEM((CHUNKS, 8) + piece, F32),
            pltpu.VMEM((CHUNKS, 5) + piece, BF16),
            pltpu.VMEM((CHUNKS, 5) + piece, BF16),
            pltpu.VMEM((CHUNKS, 2) + piece, BF16),
            pltpu.VMEM((CHUNKS, 2) + piece, BF16),
            pltpu.VMEM((2 * CHUNKS * 4,) + piece, BF16),
            pltpu.VMEM((CHUNKS, 4) + piece, BF16),
            pltpu.VMEM((CHUNKS, 4) + piece, F32),
            pltpu.VMEM((2, 16) + piece, BF16),
            pltpu.VMEM((2,) + piece, BF16),
            pltpu.SemaphoreType.DMA((6,)),
            pltpu.SemaphoreType.DMA((CHUNKS, 2)),
            pltpu.SemaphoreType.DMA((CHUNKS,)),
            pltpu.SemaphoreType.DMA((CHUNKS,)),
            pltpu.SemaphoreType.DMA((CHUNKS,)),
            pltpu.SemaphoreType.DMA((CHUNKS,)),
            pltpu.SemaphoreType.DMA((2,)),
            pltpu.SemaphoreType.DMA((CHUNKS,)),
            pltpu.SemaphoreType.DMA((CHUNKS,)),
            pltpu.SemaphoreType.DMA((CHUNKS,)),
            pltpu.SemaphoreType.DMA((CHUNKS,)),
            pltpu.SemaphoreType.DMA((CHUNKS,)),
            pltpu.SemaphoreType.DMA((CHUNKS,)),
            pltpu.SemaphoreType.DMA((2,)),
        ],
        compiler_params=pltpu.CompilerParams(
            collective_id=0, has_side_effects=True, vmem_limit_bytes=32 * 1024 * 1024
        ),
        name="relay",
    )(
        *(
            pltpu.with_memory_space_constraint(array, pltpu.HBM)
            for array in (
                w_second,
                w_first,
                hidden.reshape(CHUNKS, 4, TILE, units),
                cotangent.reshape(CHUNKS, 4, TILE, width),
                hidden,
                inputs,
            )
        )
    )
    first, second, input_grads = pl.pallas_call(
        grads_kernel,
        out_shape=(
            jax.ShapeDtypeStruct((width, units), F32),
            jax.ShapeDtypeStruct((units, width), F32),
            jax.ShapeDtypeStruct((2,) + piece, BF16),
        ),
        in_specs=[pl.BlockSpec(memory_space=pltpu.VMEM)] * 5,
        out_specs=(any_space, any_space, pl.BlockSpec(memory_space=pltpu.VMEM)),
        scratch_shapes=[
            pltpu.VMEM((width, units), F32),
            pltpu.VMEM((units, width), F32),
            pltpu.SemaphoreType.DMA((8,)),
        ],
        compiler_params=pltpu.CompilerParams(vmem_limit_bytes=24 * 1024 * 1024),
        name="weight_grads",
    )(
        inputs_t,
        activated_t,
        incoming.reshape(rows, width),
        hidden_grad.reshape(2 * rows, width),
        input_grad,
    )
    return (first[None], second[None], input_grads[None])


def solution(mesh):
    placed = (
        P("section", "wid", "hid"),
        P("section", "hid", "wid"),
        P("section", None, None, "wid"),
        P("section", None, None, "hid"),
        P(None, None, "wid"),
    )
    return jax.shard_map(
        per_device,
        mesh=mesh,
        in_specs=placed,
        out_specs=(
            P("section", "wid", "hid"),
            P("section", "hid", "wid"),
            P("section", None, "hid", "wid"),
        ),
        check_vma=False,
    )
```
